512 devices in a mesh: freq: 8 (over x, z_hi), slab: 64 (over y, z_lo, core).
Axes of the slice: x: 4, y: 8, z: 8 (z_hi: 2, z_lo: 4; z = z_hi * 4 + z_lo), core: 2. Of those that a mesh axis runs over, the one named last changes fastest.
Arguments:
- wavefield: float32 [8, 2, 2, 1024, 2048], P('freq', None, None, 'slab'), may hold values from -6 to 6
- velocity: float32 [2, 1024, 2048], P(None, 'slab', 'freq'), may hold values from 1500 to 4500
- reference_velocity: float32 [2], replicated, may hold values from 1400 to 2200
- frequencies: float32 [8], P('freq'), may hold values from 5 to 40
- block_x: float32 [8, 2, 128, 128], P('freq'), may hold values from -0.125 to 0.125
- block_y: float32 [8, 2, 128, 128], P('freq'), may hold values from -0.125 to 0.125
Outputs:
- propagated: float32 [8, 2, 2, 1024, 2048], P('freq', None, None, 'slab')
- images: float32 [2, 1024, 2048], P(None, 'slab')
The draws below stay inside these ranges and needn't reach their ends.
All inputs are finite; a program needn't handle non-finite values.
Results may differ from the reference program's by a relative error of at most 0.0003.
Values sent between devices are 32-bit elements; how exact they have to be, the bound alone decides.
A program may use at most 64 MiB of HBM per device.

```python
import math
import jax
import jax.numpy as jnp
from jax import lax

NX = 2048
NY = 1024
BLK = 128
DEPTHS = 2
FREQS = 8


def block_levels(rng, extent, split, low, top_value):
    def one(position, shards_of):
        heights = jax.random.uniform(jax.random.fold_in(jax.random.fold_in(rng, 6), position), (shards_of,), jnp.float32, low / len(split), top_value / len(split))
        return jnp.repeat(jnp.exp(heights), extent[position] // shards_of).reshape((-1,) + (1,) * (len(extent) - position - 1))

    loudness = one(*split[0])
    for cut in split[1:]:
        loudness = loudness * one(*cut)
    return loudness


def gaussian(key, extent, width, bound, cuts=(), held_as=jnp.bfloat16):
    values = jax.random.normal(key, extent, jnp.float32) * width
    if len(cuts) > 0:
        values = block_levels(key, extent, cuts, -0.22, 0.18) * values
    return jnp.clip(values, min=-bound, max=bound).astype(held_as)


def setup_inputs(seed: int = 0) -> dict:
    streams_of = jax.random.split(jax.random.key(seed), 7)
    wavefield = gaussian(streams_of[0], (FREQS, 2, 2, NY, NX), 1.0, 6.0, ((0, 8), (3, 64)), jnp.float32)
    velocity = jnp.clip(jnp.exp(math.log(4500.0) - 1.0986123 * jax.random.uniform(streams_of[1], (DEPTHS, NY, NX), jnp.float32) ** block_levels(streams_of[1], (DEPTHS, NY, NX), ((1, 64), (2, 8)), -0.2, 0.2)), 1500.0, 4500.0)
    reference_velocity = jnp.clip(jnp.exp(jax.random.uniform(streams_of[2], (DEPTHS,), jnp.float32, math.log(1400.0), math.log(2200.0))), 1400.0, 2200.0)
    frequencies = jnp.clip(5.0 + 35.0 * jax.random.uniform(streams_of[3], (FREQS,), jnp.float32) ** block_levels(streams_of[3], (FREQS,), ((0, 8),), -0.2, 0.2), 5.0, 40.0)
    block_x = gaussian(streams_of[4], (FREQS, 2, BLK, BLK), (16 * BLK) ** -0.5, 0.125, ((0, 8),), jnp.float32)
    block_y = gaussian(streams_of[5], (FREQS, 2, BLK, BLK), (16 * BLK) ** -0.5, 0.125, ((0, 8),), jnp.float32)
    return {"wavefield": wavefield, "velocity": velocity, "reference_velocity": reference_velocity, "frequencies": frequencies, "block_x": block_x, "block_y": block_y}


spacing = 12.5
depth_step = 10.0

def wavenumbers(length):
    counter = jnp.arange(length, dtype=jnp.int32)
    signed = jnp.where(counter >= length // 2, counter - length, counter)
    return 2.0 * math.pi * signed.astype(jnp.float32) / (length * spacing)

def correct_last(field, strength, blocks):
    padded = jnp.pad(field, ((0, 0), (0, 0), (1, 1)))
    curvature = padded[:, :, 2:] - 2.0 * field + padded[:, :, :-2]
    mixed = field + 1j * strength * curvature
    size_block = blocks.shape[-1]
    tiles = mixed.reshape(mixed.shape[0], mixed.shape[1], mixed.shape[2] // size_block, size_block)
    matrix = blocks[0] + 1j * blocks[1]
    added = jnp.einsum('grni,ji->grnj', tiles, matrix, precision=lax.Precision.HIGHEST)
    return (tiles + added).reshape(field.shape)

def correct_along_y(current, strength, blocks):
    turned = jnp.swapaxes(current, 1, 2)
    return jnp.swapaxes(correct_last(turned, strength.T, blocks), 1, 2)

def reference(wavefield, velocity, reference_velocity, frequencies, block_x, block_y):
    wave_x = wavenumbers(NX)
    wave_y = wavenumbers(NY)

    def one_frequency(inputs):
        field_pair, frequency, blocks_x, blocks_y = inputs
        angular = 2.0 * math.pi * frequency
        current = field_pair[:, 0] + 1j * field_pair[:, 1]
        pictures = []
        for depth_index in range(DEPTHS):
            speed = velocity[depth_index]
            ref_speed = reference_velocity[depth_index]
            vertical = (angular / ref_speed) ** 2 - wave_x[None, :] ** 2 - wave_y[:, None] ** 2
            magnitude = jnp.sqrt(jnp.abs(vertical))
            travels = vertical >= 0
            multiplier = jnp.where(travels, jnp.exp(1j * depth_step * magnitude), jnp.exp(-depth_step * magnitude))
            spectrum = jnp.fft.fft2(current, axes=(1, 2))
            current = jnp.fft.ifft2(spectrum * multiplier[None], axes=(1, 2))
            current = current * jnp.exp(1j * angular * depth_step * (1.0 / speed - 1.0 / ref_speed))[None]
            strength = 0.5 * (1.0 - ref_speed / speed)
            if depth_index % 2 == 0:
                current = correct_last(current, strength, blocks_x)
                current = correct_along_y(current, strength, blocks_y)
            else:
                current = correct_along_y(current, strength, blocks_y)
                current = correct_last(current, strength, blocks_x)
            pictures.append(jnp.real(current[0] * current[1]))
        fields = jnp.stack((jnp.real(current), jnp.imag(current)), axis=1)
        return (fields, jnp.stack(pictures))
    fields, pictures = lax.map(one_frequency, (wavefield, frequencies, block_x, block_y))
    images = lax.optimization_barrier(jnp.sum(pictures, axis=0)).astype(jnp.float32)
    return (fields, images)
```

```python
import functools
import math

import jax
import jax.numpy as jnp
import numpy as np
from jax import lax
from jax.experimental import pallas as pl
from jax.experimental.pallas import tpu as pltpu
from jax.sharding import PartitionSpec as P

F32 = jnp.float32
BF16 = jnp.bfloat16
MESH = pl.DeviceIdType.MESH

NX = 2048
NY = 1024
SLABS = 64
GROUPS = 8
ROWS = 16
spacing = 12.5
depth_step = 10.0


def split_table(table):
    high = table.astype(jnp.bfloat16)
    low = (table - high.astype(np.float64)).astype(jnp.bfloat16)
    return high, low


def angle(product, period):
    turns = 2.0 * math.pi * (product % period) / period
    return np.cos(turns), -np.sin(turns)


@functools.lru_cache(maxsize=None)
def tables():
    sixteen = np.arange(16)
    cos, sin = angle(sixteen[:, None] * sixteen[None, :], 16)
    eye = np.eye(ROWS)
    left_x = np.concatenate([np.kron(cos, eye), np.kron(sin, eye)], 1)
    index = np.arange(256)
    left_y = np.concatenate(angle(index[:, None] * index[None, :], 256), 1)
    lefts = []
    for table in (left_x, left_y):
        high, low = split_table(table)
        lefts.append(np.concatenate([high, high, low], 1))
    inner = np.arange(128)
    cos, sin = angle(inner[:, None] * inner[None, :], 128)
    full = np.zeros((4, 2, 2, 32, 4, 2, 2, 32))
    for field in range(2):
        for c, d, block in ((0, 0, cos), (0, 1, sin), (1, 0, -sin), (1, 1, cos)):
            full[:, c, field, :, :, d, field, :] = block.reshape(4, 32, 4, 32)
    high, low = split_table(full.reshape(512, 512))
    right_x = np.concatenate([high, high, low], 0)
    quarter, outer, column = np.arange(4), np.arange(16), np.arange(32)
    position = quarter[:, None] * 32 + column[None, :]
    product = outer[None, :, None] * position[:, None, :]
    twist_x = []
    for part in angle(product, NX):
        part = np.broadcast_to(part[:, :, None, None, :], (4, 16, 16, 4, 32))
        twist_x.append(part.reshape(1024, 128).astype(np.float32))
    product = np.arange(4)[:, None] * np.arange(256)[None, :]
    twist_y = []
    for part in angle(product, NY):
        part = np.broadcast_to(part.reshape(1024, 1), (1024, 128))
        twist_y.append(part.astype(np.float32))
    return (lefts[0], lefts[1], right_x, *twist_x, *twist_y)


def lanes(rows=1):
    return lax.broadcasted_iota(jnp.int32, (rows, 128), 1)


def turn(x):
    sign = jnp.where(lanes() < 64, -1.0, 1.0)
    return pltpu.roll(x, 64, 1) * sign


def conjugate(x):
    return x * jnp.where(lanes() < 64, 1.0, -1.0)


def halves(x):
    high = x.astype(BF16)
    return high, (x - high.astype(F32)).astype(BF16)


def left_product(table_ref, blocks, direction):
    columns = []
    for x in blocks:
        y = turn(x) * direction if direction != 1 else turn(x)
        high_x, low_x = halves(x)
        high_y, low_y = halves(y)
        columns.append(jnp.concatenate([high_x, high_y, low_x, low_y, high_x, high_y], 0))
    operand = jnp.concatenate(columns, 1)
    total = jnp.dot(table_ref[...], operand, preferred_element_type=F32)
    return [total[:, 128 * k : 128 * (k + 1)] for k in range(len(blocks))]


def right_product(table_ref, blocks):
    highs, lows = zip(*[halves(x) for x in blocks])
    operand = jnp.concatenate([*highs, *lows, *highs], 1)
    total = jnp.dot(operand, table_ref[...], preferred_element_type=F32)
    return [total[:, 128 * k : 128 * (k + 1)] for k in range(4)]


def rotated(x, factor_real, factor_imag):
    return x * factor_real + turn(x) * factor_imag


def at(start, size, unit):
    return pl.ds(pl.multiple_of(start, unit), size)


def outer_x(source, target, left_ref, twist, direction):
    def step(i, carry):
        rows = [at(512 * i + 256 * k, 256, 256) for k in range(2)]
        blocks = [source[r, :] for r in rows]
        if direction < 0:
            blocks = [rotated(b, twist[0][r, :], -twist[1][r, :]) for b, r in zip(blocks, rows)]
        blocks = left_product(left_ref, blocks, direction)
        if direction > 0:
            blocks = [rotated(b, twist[0][r, :], twist[1][r, :]) for b, r in zip(blocks, rows)]
        for b, r in zip(blocks, rows):
            target[r, :] = b
        return carry

    lax.fori_loop(0, 2, step, 0)


def inner_x(source, target, right_ref, before, after):
    def step(i, carry):
        rows = [at(256 * k + 128 * i, 128, 128) for k in range(4)]
        blocks = right_product(right_ref, [before(source[r, :], r) for r in rows])
        for b, r in zip(blocks, rows):
            target[r, :] = after(b, r)
        return carry

    lax.fori_loop(0, 2, step, 0)


def forward_y(source, target, left_ref, twist):
    def butterfly(i, carry):
        rows = [at(256 * k + 32 * i, 32, 32) for k in range(4)]
        x0, x1, x2, x3 = [source[r, :] for r in rows]
        even, odd = x0 + x2, x1 + x3
        minus, spun = x0 - x2, turn(x1 - x3)
        results = [even + odd, minus - spun, even - odd, minus + spun]
        for k, r in enumerate(rows):
            value = results[k]
            if k > 0:
                value = rotated(value, twist[0][r, :], twist[1][r, :])
            target[r, :] = value
        return carry

    lax.fori_loop(0, 8, butterfly, 0)
    middle_y(target, target, left_ref, 1)


def middle_y(source, target, left_ref, direction):
    def step(i, carry):
        rows = [at(512 * i + 256 * k, 256, 256) for k in range(2)]
        blocks = left_product(left_ref, [source[r, :] for r in rows], direction)
        for b, r in zip(blocks, rows):
            target[r, :] = b
        return carry

    lax.fori_loop(0, 2, step, 0)


def inverse_y(source, target, left_ref, twist, finish):
    middle_y(source, source, left_ref, -1)

    def butterfly(i, carry):
        rows = [at(256 * k + 32 * i, 32, 32) for k in range(4)]
        x0, x1, x2, x3 = [source[r, :] for r in rows]
        x1, x2, x3 = [
            rotated(x, twist[0][r, :], -twist[1][r, :]) for x, r in zip((x1, x2, x3), rows[1:])
        ]
        even, odd = x0 + x2, x1 + x3
        minus, spun = x0 - x2, turn(x1 - x3)
        results = [even + odd, minus + spun, even - odd, minus - spun]
        for value, r in zip(results, rows):
            target[r, :] = finish(value, r)
        return carry

    lax.fori_loop(0, 8, butterfly, 0)


def series(square, first):
    value = jnp.full_like(square, (-1.0) ** 8 / math.factorial(16 + first))
    for n in range(7, -1, -1):
        value = value * square + (-1.0) ** n / math.factorial(2 * n + first)
    return value


def wavenumber(index, length):
    signed = jnp.where(index >= length // 2, index - length, index)
    return signed.astype(F32) * (2.0 * math.pi / (length * spacing))


def phase_factors(target_real, target_imag, ratio_square, positions):
    def step(i, carry):
        r = at(64 * i, 64, 64)
        row = lax.broadcasted_iota(jnp.int32, (64, 128), 0) + 64 * i
        column = lanes(64) % 32
        index_x, index_y = positions(row, column)
        wave_x, wave_y = wavenumber(index_x, NX), wavenumber(index_y, NY)
        vertical = ratio_square - wave_x * wave_x - wave_y * wave_y
        square = jnp.abs(vertical) * (depth_step * depth_step)
        size = jnp.sqrt(square)
        travels = vertical >= 0
        scale = 1.0 / (NX * NY)
        target_real[r, :] = jnp.where(travels, series(square, 0), jnp.exp(-size)) * scale
        target_imag[r, :] = jnp.where(travels, size * series(square, 1), 0.0) * scale
        return carry

    lax.fori_loop(0, 16, step, 0)


def split_factors(speed, ref_speed, angular):
    turned = angular * depth_step * (1.0 / speed - 1.0 / ref_speed)
    square = turned * turned
    return series(square, 0), turned * series(square, 1)


def strength_of(speed, ref_speed):
    return 0.5 * (1.0 - ref_speed / speed)


def spread(x, group):
    x = jnp.where(lanes() // 32 == group, x, 0.0)
    x = x + pltpu.roll(x, 64, 1)
    return x + pltpu.roll(x, 32, 1)


def regroup(blocks, index):
    group = lanes() // 32
    result = jnp.zeros_like(blocks[0])
    for g, x in enumerate(blocks):
        shift = 32 * (g - index) % 128
        result = jnp.where(group == g, pltpu.roll(x, shift, 1) if shift else x, result)
    return result


def correct_x(source, padded, mixed, target, strength_ref, right_ref):
    padded[256:1280, :] = source[...]
    padded[0:16, :] = jnp.zeros((16, 128), F32)
    padded[16:256, :] = source[768:1008, :]
    padded[1280:1520, :] = source[16:256, :]
    padded[1520:1536, :] = jnp.zeros((16, 128), F32)
    column = lanes() % 32

    def step(i, carry):
        x = padded[at(256 + 64 * i, 64, 64), :]
        behind = pltpu.roll(padded[at(64 * i, 64, 64), :], 97, 1)
        ahead = pltpu.roll(padded[at(512 + 64 * i, 64, 64), :], 31, 1)
        before = jnp.where(column == 0, behind, pltpu.roll(x, 1, 1))
        after = jnp.where(column == 31, ahead, pltpu.roll(x, 127, 1))
        curvature = before + after - 2.0 * x
        r = at(64 * i, 64, 64)
        mixed[r, :] = x + turn(curvature) * strength_ref[r, :]
        return carry

    lax.fori_loop(0, 16, step, 0)
    inner_x(mixed, target, right_ref, lambda x, r: x, lambda x, r: x + mixed[r, :])


def correct_y(padded, mixed, target, strength_ref, left_ref):
    for i in range(8):
        x = padded[8 + 128 * i : 136 + 128 * i, :]
        before = padded[7 + 128 * i : 135 + 128 * i, :]
        after = padded[9 + 128 * i : 137 + 128 * i, :]
        curvature = before + after - 2.0 * x
        r = slice(128 * i, 128 * i + 128)
        mixed[r, :] = x + turn(curvature) * strength_ref[r, :]

    def step(i, carry):
        rows = [at(256 * i + 128 * k, 128, 128) for k in range(2)]
        blocks = [mixed[r, :] for r in rows]
        added = left_product(left_ref, blocks, 1)
        for x, b, r in zip(blocks, added, rows):
            target[r, :] = x + b
        return carry

    lax.fori_loop(0, 4, step, 0)


def build_blocks(bx_ref, by_ref, right_ref, left_ref):
    for k in range(2):
        high, low = halves(by_ref[0, k])
        for place, value in ((k, high), (2 + k, high), (4 + k, low)):
            left_ref[:, 128 * place : 128 * (place + 1)] = value
    real, imag = bx_ref[0, 0].T, bx_ref[0, 1].T
    zero = jnp.zeros_like(real)
    for c in range(2):
        pair = (real, imag) if c == 0 else (-imag, real)
        for field in range(2):
            blocks = [zero] * 4
            blocks[field], blocks[2 + field] = pair
            for quarter in range(4):
                high, low = halves(regroup(blocks, quarter))
                for q in range(4):
                    base = 128 * q + 64 * c + 32 * field
                    for offset, value in ((0, high), (512, high), (1024, low)):
                        right_ref[offset + base : offset + base + 32, 128 * quarter : 128 * (quarter + 1)] = value[
                            32 * q : 32 * q + 32
                        ]


def kernel(
    refv_ref,
    freq_ref,
    wave_ref,
    vel_ref,
    bx_ref,
    by_ref,
    left_x,
    left_y,
    right_x,
    twist_xr,
    twist_xi,
    twist_yr,
    twist_yi,
    out_ref,
    image_ref,
    sent,
    got,
    work_a,
    work_b,
    padded_x,
    padded_y,
    block_right,
    block_left,
    phase_real,
    phase_imag,
    turn_real,
    turn_imag,
    strength_x,
    strength_y,
    vel_all,
    vel_sent,
    vel_got,
    img_sent,
    img_got,
    part,
    shares,
    summed,
    totals,
    send_sem,
    recv_sem,
    small_send,
    small_recv,
    freq_send,
    freq_recv,
):
    group = lax.axis_index("freq")
    me = lax.axis_index("slab")

    barrier = pltpu.get_barrier_semaphore()

    def greet_slab(i, carry):
        pl.semaphore_signal(barrier, inc=1, device_id=(group, lax.rem(me + i, SLABS)), device_id_type=MESH)
        return carry

    def greet_freq(i, carry):
        pl.semaphore_signal(barrier, inc=1, device_id=(lax.rem(group + i, GROUPS), me), device_id_type=MESH)
        return carry

    lax.fori_loop(1, GROUPS, greet_freq, 0)
    lax.fori_loop(1, SLABS, greet_slab, 0)

    def exchange(source, landing, rows, send, recv):
        own = at(me * rows, rows, rows)

        def step(i, carry):
            other = lax.rem(me + i, SLABS)
            pltpu.make_async_remote_copy(
                src_ref=source.at[at(other * rows, rows, rows), :],
                dst_ref=landing.at[own, :],
                send_sem=send,
                recv_sem=recv,
                device_id=(group, other),
                device_id_type=MESH,
            ).start()
            return carry

        pltpu.make_async_copy(source.at[own, :], landing.at[own, :], recv).start()
        lax.fori_loop(1, SLABS, step, 0)

    def arrived(landing, recv):
        pltpu.make_async_copy(landing, landing, recv).wait()

    def left_here(source, rows, send):
        count = rows * (SLABS - 1)
        pltpu.make_async_copy(source.at[0:count, :], source.at[0:count, :], send).wait()

    def share(piece, landing, send, recv):
        def step(i, carry):
            other = lax.rem(group + i, GROUPS)
            pltpu.make_async_remote_copy(
                src_ref=piece(other),
                dst_ref=landing.at[group],
                send_sem=send,
                recv_sem=recv,
                device_id=(other, me),
                device_id_type=MESH,
            ).start()
            return carry

        pltpu.make_async_copy(piece(group), landing.at[group], recv).start()
        lax.fori_loop(1, GROUPS, step, 0)

    def shared_left(landing, send):
        pltpu.make_async_copy(landing.at[0 : GROUPS - 1], landing.at[0 : GROUPS - 1], send).wait()

    def field_out(k):
        exchange(sent.at[k], got.at[k], ROWS, send_sem.at[k], recv_sem.at[k])

    def field_in(k):
        arrived(got.at[k], recv_sem.at[k])

    def pack(a, carry):
        window = at(a * 128, 128, 128)
        blocks = [wave_ref[0, g % 2, g // 2, :, window] for g in range(4)]
        for q in range(4):
            work_a[at(q * 256 + a * 16, 16, 16), :] = regroup(blocks, q)
        return carry

    lax.fori_loop(0, 16, pack, 0)
    twist_x = (twist_xr, twist_xi)
    twist_y = (twist_yr, twist_yi)
    outer_x(work_a, work_b, left_x, twist_x, 1)
    inner_x(work_b, sent.at[0], right_x, lambda x, r: x, lambda x, r: x)

    pl.semaphore_wait(barrier, SLABS - 1 + GROUPS - 1)
    field_out(0)
    share(lambda g: vel_ref, vel_all, freq_send.at[0], freq_recv.at[0])

    angular = jnp.full((1, 128), freq_ref[0], F32) * (2.0 * math.pi)
    speeds = [jnp.full((1, 128), refv_ref[d], F32) for d in range(2)]
    squares = [(angular / v) * (angular / v) for v in speeds]

    def positions_y(row, column):
        index_x = lax.rem(me, 16) + 16 * (lax.div(me, 16) * 32 + column)
        return index_x, row // 256 + 4 * (row % 256)

    phase_factors(phase_real.at[0], phase_imag.at[0], squares[0], positions_y)
    build_blocks(bx_ref, by_ref, block_right, block_left)

    arrived(vel_all, freq_recv.at[0])

    def pack_speed(a, carry):
        f = lax.div(a, 2)
        window = at(lax.rem(a, 2) * 128, 128, 128)
        for d in range(2):
            x = vel_all[f, d, :, window]
            for q in range(4):
                r = at(q * 256 + a * 16, 16, 16)
                speed = spread(x, q)
                strength_x[d, r, :] = strength_of(speed, speeds[d])
                if d == 0:
                    real, imag = split_factors(speed, speeds[d], angular)
                    turn_real[0, r, :] = real
                    turn_imag[0, r, :] = imag
        blocks = [vel_all[f, g % 2, 8 * (g // 2) : 8 * (g // 2) + 8, window] for g in range(4)]
        for q in range(4):
            vel_sent[at((q * 16 + a) * 8, 8, 8), :] = regroup(blocks, q)
        return carry

    lax.fori_loop(0, 16, pack_speed, 0)
    exchange(vel_sent, vel_got, 8, small_send.at[0], small_recv.at[0])

    field_in(0)
    forward_y(got.at[0], work_a, left_y, twist_y)

    def shift(source, target, k):
        def step(i, carry):
            r = at(64 * i, 64, 64)
            target[r, :] = rotated(source[r, :], phase_real[k, r, :], phase_imag[k, r, :])
            return carry

        lax.fori_loop(0, 16, step, 0)

    shift(work_a, work_b, 0)
    inverse_y(work_b, sent.at[1], left_y, twist_y, lambda x, r: x)
    field_out(1)

    arrived(vel_got, small_recv.at[0])

    def unpack_speed(s, carry):
        x = vel_got[at(8 * s, 8, 8), :]
        for d in range(2):
            for h in range(2):
                r = at(16 * s + 8 * h, 8, 8)
                speed = spread(x, 2 * h + d)
                strength_y[d, r, :] = strength_of(speed, speeds[d])
                if d == 1:
                    real, imag = split_factors(speed, speeds[d], angular)
                    turn_real[1, r, :] = real
                    turn_imag[1, r, :] = imag
        return carry

    lax.fori_loop(0, 64, unpack_speed, 0)

    def positions_x(row, column):
        line = me * 16 + row % 16
        index_x = row // 16 % 16 + 16 * (row // 256 * 32 + column)
        return index_x, line // 256 + 4 * (line % 256)

    phase_factors(phase_real.at[1], phase_imag.at[1], squares[1], positions_x)

    field_in(1)
    inner_x(got.at[1], work_a, right_x, lambda x, r: conjugate(x), lambda x, r: conjugate(x))
    outer_x(work_a, work_b, left_x, twist_x, -1)

    def split_x(i, carry):
        r = at(64 * i, 64, 64)
        work_a[r, :] = rotated(work_b[r, :], turn_real[0, r, :], turn_imag[0, r, :])
        return carry

    lax.fori_loop(0, 16, split_x, 0)
    correct_x(work_a, padded_x, work_b, sent.at[2], strength_x.at[0], block_right)
    field_out(2)

    zeros = jnp.zeros((8, 128), F32)
    padded_y[0:8, :] = zeros
    padded_y[1032:1040, :] = zeros
    field_in(2)
    padded_y[8:1032, :] = got[2]
    correct_y(padded_y, work_a, work_b, strength_y.at[0], block_left)

    forward_y(work_b, sent.at[3], left_y, twist_y)
    field_out(3)

    def image_y(s, carry):
        group_of = lanes() // 32
        pieces = []
        for h in range(2):
            x = work_b[at(16 * s + 8 * h, 8, 8), :]
            product = x * pltpu.roll(x, 96, 1)
            pieces.append(product - pltpu.roll(product, 64, 1))
        packed = jnp.where(group_of == 1, pltpu.roll(pieces[1], 32, 1), 0.0)
        img_sent[at(8 * s, 8, 8), :] = jnp.where(group_of == 0, pieces[0], packed)
        return carry

    lax.fori_loop(0, 64, image_y, 0)
    exchange(img_sent, img_got, 8, small_send.at[1], small_recv.at[1])

    field_in(3)
    outer_x(got.at[3], work_a, left_x, twist_x, 1)

    def shifted(x, r):
        return conjugate(rotated(x, phase_real[1, r, :], phase_imag[1, r, :]))

    inner_x(work_a, work_b, right_x, lambda x, r: x, shifted)
    inner_x(work_b, work_a, right_x, lambda x, r: x, lambda x, r: conjugate(x))
    outer_x(work_a, sent.at[4], left_x, twist_x, -1)
    field_out(4)

    def reduce_out(d):
        share(lambda g: part.at[d, at(2 * g, 2, 2)], shares.at[d], freq_send.at[1 + d], freq_recv.at[1 + d])

    def gather_out(d):
        arrived(shares.at[d], freq_recv.at[1 + d])
        total = shares[d, 0]
        for g in range(1, GROUPS):
            total = total + shares[d, g]
        summed[d] = total
        share(lambda g: summed.at[d], totals.at[d], freq_send.at[3 + d], freq_recv.at[3 + d])

    arrived(img_got, small_recv.at[1])

    def image_x(a, carry):
        group_of = lanes() // 32
        for h in range(2):
            result = jnp.zeros((8, 128), F32)
            for q in range(4):
                x = img_got[at((q * 16 + a) * 8, 8, 8), :]
                amount = 32 * (q - h) % 128
                result = jnp.where(group_of == q, pltpu.roll(x, amount, 1) if amount else x, result)
            part[0, a, 8 * h : 8 * h + 8, :] = result
        return carry

    lax.fori_loop(0, 16, image_x, 0)
    reduce_out(0)

    field_in(4)

    def split_y(x, r):
        return rotated(x, turn_real[1, r, :], turn_imag[1, r, :])

    def copy_in(i, carry):
        r = at(64 * i, 64, 64)
        work_b[r, :] = got[4, r, :]
        return carry

    lax.fori_loop(0, 16, copy_in, 0)
    inverse_y(work_b, work_a, left_y, twist_y, split_y)
    padded_y[8:1032, :] = work_a[...]
    correct_y(padded_y, work_b, sent.at[5], strength_y.at[1], block_left)
    field_out(5)
    gather_out(0)

    field_in(5)
    correct_x(got.at[5], padded_x, work_b, work_a, strength_x.at[1], block_right)

    def image_last(a, carry):
        blocks = [work_a[at(q * 256 + a * 16, 16, 16), :] for q in range(4)]
        whole = [regroup(blocks, g) for g in range(4)]
        part[1, a] = whole[0] * whole[1] - whole[2] * whole[3]
        window = at(a * 128, 128, 128)
        for g in range(4):
            out_ref[0, g % 2, g // 2, :, window] = whole[g]
        return carry

    lax.fori_loop(0, 16, image_last, 0)
    reduce_out(1)
    gather_out(1)

    for d in range(2):
        arrived(totals.at[d], freq_recv.at[3 + d])
        for a in range(16):
            image_ref[d, :, 128 * a : 128 * (a + 1)] = totals[d, a // 2, a % 2]

    for k in range(6):
        left_here(sent.at[k], ROWS, send_sem.at[k])
    left_here(vel_sent, 8, small_send.at[0])
    left_here(img_sent, 8, small_send.at[1])
    shared_left(vel_all, freq_send.at[0])
    for d in range(2):
        shared_left(shares.at[d], freq_send.at[1 + d])
        shared_left(totals.at[d], freq_send.at[3 + d])


def body(wavefield, velocity, reference_velocity, frequencies, block_x, block_y):
    state = (1024, 128)
    vmem, smem = pl.BlockSpec(memory_space=pltpu.VMEM), pl.BlockSpec(memory_space=pltpu.SMEM)
    constants = [jnp.asarray(t) for t in tables()]
    call = pl.pallas_call(
        kernel,
        out_shape=(
            jax.ShapeDtypeStruct(wavefield.shape, F32),
            jax.ShapeDtypeStruct((2, ROWS, NX), F32),
        ),
        in_specs=[smem, smem] + [vmem] * (4 + len(constants)),
        out_specs=(vmem, vmem),
        scratch_shapes=[
            pltpu.VMEM((6, *state), F32),
            pltpu.VMEM((6, *state), F32),
            pltpu.VMEM(state, F32),
            pltpu.VMEM(state, F32),
            pltpu.VMEM((1536, 128), F32),
            pltpu.VMEM((1040, 128), F32),
            pltpu.VMEM((1536, 512), BF16),
            pltpu.VMEM((128, 768), BF16),
            pltpu.VMEM((2, *state), F32),
            pltpu.VMEM((2, *state), F32),
            pltpu.VMEM((2, *state), F32),
            pltpu.VMEM((2, *state), F32),
            pltpu.VMEM((2, *state), F32),
            pltpu.VMEM((2, *state), F32),
            pltpu.VMEM((GROUPS, 2, ROWS, 256), F32),
            pltpu.VMEM((512, 128), F32),
            pltpu.VMEM((512, 128), F32),
            pltpu.VMEM((512, 128), F32),
            pltpu.VMEM((512, 128), F32),
            pltpu.VMEM((2, 16, ROWS, 128), F32),
            pltpu.VMEM((2, GROUPS, 2, ROWS, 128), F32),
            pltpu.VMEM((2, 2, ROWS, 128), F32),
            pltpu.VMEM((2, GROUPS, 2, ROWS, 128), F32),
            pltpu.SemaphoreType.DMA((6,)),
            pltpu.SemaphoreType.DMA((6,)),
            pltpu.SemaphoreType.DMA((2,)),
            pltpu.SemaphoreType.DMA((2,)),
            pltpu.SemaphoreType.DMA((5,)),
            pltpu.SemaphoreType.DMA((5,)),
        ],
        compiler_params=pltpu.CompilerParams(
            collective_id=0, has_side_effects=True, vmem_limit_bytes=48 * 1024 * 1024
        ),
    )
    return call(reference_velocity, frequencies, wavefield, velocity, block_x, block_y, *constants)


def solution(mesh):
    in_specs = (
        P("freq", None, None, "slab", None),
        P(None, "slab", "freq"),
        P(),
        P("freq"),
        P("freq", None, None, None),
        P("freq", None, None, None),
    )
    out_specs = (P("freq", None, None, "slab", None), P(None, "slab", None))
    return jax.shard_map(body, mesh=mesh, in_specs=in_specs, out_specs=out_specs, check_vma=False)
```

```python
import functools
import math

import jax
import jax.numpy as jnp
import numpy as np
from jax import lax
from jax.experimental import pallas as pl
from jax.experimental.pallas import tpu as pltpu
from jax.sharding import PartitionSpec as P

F32 = jnp.float32
BF16 = jnp.bfloat16
MESH = pl.DeviceIdType.MESH

NX = 2048
NY = 1024
SLABS = 64
GROUPS = 8
HALF = 8
STRIDE = 27
spacing = 12.5
depth_step = 10.0


def split_table(table):
    high = table.astype(jnp.bfloat16)
    low = (table - high.astype(np.float64)).astype(jnp.bfloat16)
    return high, low


def angle(product, period):
    turns = 2.0 * math.pi * (product % period) / period
    return np.cos(turns), -np.sin(turns)


@functools.lru_cache(maxsize=None)
def tables():
    sixteen = np.arange(16)
    cos, sin = angle(sixteen[:, None] * sixteen[None, :], 16)
    eye = np.eye(HALF)
    high, low = split_table(np.concatenate([np.kron(cos, eye), np.kron(sin, eye)], 1))
    left_x = np.concatenate([high, high, low], 1)
    place = np.arange(16)[:, None] * 16 + np.arange(8)[None, :]
    places = [(place + 8 * h).reshape(128) for h in range(2)]
    order = np.concatenate(places)
    left_y = []
    for h in range(2):
        high, low = split_table(np.concatenate(angle(order[:, None] * places[h][None, :], 256), 1))
        left_y.append(np.concatenate([high, high, low], 1))
    left_y = np.stack(left_y)
    inner = np.arange(128)
    cos, sin = angle(inner[:, None] * inner[None, :], 128)
    full = np.zeros((4, 2, 2, 32, 4, 2, 2, 32))
    for field in range(2):
        for c, d, block in ((0, 0, cos), (0, 1, sin), (1, 0, -sin), (1, 1, cos)):
            full[:, c, field, :, :, d, field, :] = block.reshape(4, 32, 4, 32)
    right_x = np.concatenate(split_table(full.reshape(512, 512)), 0)
    quarter, outer, column = np.arange(4), np.arange(16), np.arange(32)
    position = quarter[:, None] * 32 + column[None, :]
    product = outer[None, :, None] * position[:, None, :]
    twist_x = []
    for part in angle(product, NX):
        part = np.broadcast_to(part[:, :, None, None, :], (4, 16, HALF, 4, 32))
        twist_x.append(part.reshape(512, 128))
    product = np.arange(4)[None, :, None] * np.stack(places)[:, None, :]
    twist_y = []
    for part in angle(product, NY):
        part = np.broadcast_to(part.reshape(2, 512, 1), (2, 512, 128))
        twist_y.append(part)
    return left_x, np.stack(twist_x).astype(np.float32), right_x, left_y, np.stack(twist_y).astype(np.float32)


def lanes(rows=1):
    return lax.broadcasted_iota(jnp.int32, (rows, 128), 1)


def turn(x):
    sign = jnp.where(lanes() < 64, -1.0, 1.0)
    return pltpu.roll(x, 64, 1) * sign


def unturn(x):
    sign = jnp.where(lanes() < 64, 1.0, -1.0)
    return pltpu.roll(x, 64, 1) * sign


def conjugate(x):
    return x * jnp.where(lanes() < 64, 1.0, -1.0)


def halves(x):
    high = x.astype(BF16)
    return high, (x - high.astype(F32)).astype(BF16)


def left_operand(blocks, direction):
    columns = []
    for x in blocks:
        y = turn(x) if direction > 0 else unturn(x)
        high_x, low_x = halves(x)
        high_y, low_y = halves(y)
        columns.append(jnp.concatenate([high_x, high_y, low_x, low_y, high_x, high_y], 0))
    return jnp.concatenate(columns, 1)


def product(left, right):
    return jnp.dot(left, right, preferred_element_type=F32)


def in_blocks(total):
    return [total[:, 128 * k : 128 * (k + 1)] for k in range(total.shape[1] // 128)]


def right_product(table_ref, blocks):
    highs, lows = zip(*[halves(x) for x in blocks])
    return in_blocks(product(jnp.concatenate([*highs, *highs, *lows], 1), table_ref[...]))


def rotated(x, factor_real, factor_imag):
    return x * factor_real + turn(x) * factor_imag


def rotated_back(x, factor_real, factor_imag):
    return x * factor_real + unturn(x) * factor_imag


def at(start, size, unit):
    return pl.ds(pl.multiple_of(start, unit), size)


def quarters(ref):
    return [ref[128 * k : 128 * (k + 1), :] for k in range(4)]


def put(ref, blocks):
    for k, x in enumerate(blocks):
        ref[128 * k : 128 * (k + 1), :] = x


def outer_x(blocks, left_ref, twist, direction):
    rows = [slice(128 * k, 128 * (k + 1)) for k in range(4)]
    if direction < 0:
        blocks = [rotated_back(b, twist[0, r, :], twist[1, r, :]) for b, r in zip(blocks, rows)]
    blocks = in_blocks(product(left_ref[...], left_operand(blocks, direction)))
    if direction > 0:
        blocks = [rotated(b, twist[0, r, :], twist[1, r, :]) for b, r in zip(blocks, rows)]
    return blocks


def inverse_inner_x(blocks, right_ref):
    return [conjugate(b) for b in right_product(right_ref, [conjugate(b) for b in blocks])]


def butterfly_forward(source, target, twist, h):
    def step(i, carry):
        rows = [at(128 * k + 32 * i, 32, 32) for k in range(4)]
        x0, x1, x2, x3 = [source[r, :] for r in rows]
        even, odd = x0 + x2, x1 + x3
        minus, spun = x0 - x2, turn(x1 - x3)
        results = [even + odd, minus - spun, even - odd, minus + spun]
        for k, r in enumerate(rows):
            value = results[k]
            if k > 0:
                value = rotated(value, twist[0, h, r, :], twist[1, h, r, :])
            target[r, :] = value
        return carry

    lax.fori_loop(0, 4, step, 0)


def butterfly_inverse(source, target, twist, h, finish):
    def step(i, carry):
        rows = [at(128 * k + 32 * i, 32, 32) for k in range(4)]
        x0, x1, x2, x3 = [source[r, :] for r in rows]
        x1, x2, x3 = [
            rotated_back(x, twist[0, h, r, :], twist[1, h, r, :])
            for x, r in zip((x1, x2, x3), rows[1:])
        ]
        even, odd = x0 + x2, x1 + x3
        minus, spun = x0 - x2, turn(x1 - x3)
        results = [even + odd, minus + spun, even - odd, minus - spun]
        for value, r in zip(results, rows):
            target[r, :] = finish(value, r)
        return carry

    lax.fori_loop(0, 4, step, 0)


def series(square, first):
    value = jnp.full_like(square, 1.0 / math.factorial(16 + first))
    for n in range(7, -1, -1):
        value = value * square + (-1.0) ** n / math.factorial(2 * n + first)
    return value


def wavenumber(index, length):
    signed = jnp.where(index >= length // 2, index - length, index)
    return signed.astype(F32) * (2.0 * math.pi / (length * spacing))


def phase_factors(target_real, target_imag, ratio_square, positions):
    def step(i, carry):
        r = at(64 * lax.rem(i, 8), 64, 64)
        h = lax.div(i, 8)
        row = lax.broadcasted_iota(jnp.int32, (64, 128), 0) + 64 * lax.rem(i, 8)
        column = lanes(64) % 32
        index_x, index_y = positions(h, row, column)
        wave_x, wave_y = wavenumber(index_x, NX), wavenumber(index_y, NY)
        vertical = ratio_square - wave_x * wave_x - wave_y * wave_y
        square = jnp.abs(vertical) * (depth_step * depth_step)
        size = jnp.sqrt(square)
        travels = vertical >= 0
        scale = 1.0 / (NX * NY)
        target_real[h, r, :] = jnp.where(travels, series(square, 0), jnp.exp(-size)) * scale
        target_imag[h, r, :] = jnp.where(travels, size * series(square, 1), 0.0) * scale
        return carry

    lax.fori_loop(0, 16, step, 0)


def split_factors(speed, ref_speed, angular):
    turned = angular * depth_step * (1.0 / speed - 1.0 / ref_speed)
    square = turned * turned
    return series(square, 0), turned * series(square, 1)


def strength_of(speed, ref_speed):
    return 0.5 * (1.0 - ref_speed / speed)


def spread(x, group):
    x = jnp.where(lanes() // 32 == group, x, 0.0)
    x = x + pltpu.roll(x, 64, 1)
    return x + pltpu.roll(x, 32, 1)


def regroup(blocks, index):
    group = lanes() // 32
    result = jnp.zeros_like(blocks[0])
    for g, x in enumerate(blocks):
        shift = 32 * (g - index) % 128
        result = jnp.where(group == g, pltpu.roll(x, shift, 1) if shift else x, result)
    return result


def correct_x(blocks, padded, strength, right_ref):
    for k in range(4):
        padded[128 * (k + 1) : 128 * (k + 2), :] = blocks[k]
    padded[0:8, :] = jnp.zeros((8, 128), F32)
    padded[8:128, :] = blocks[3][0:120]
    padded[640:760, :] = blocks[0][8:128]
    padded[760:768, :] = jnp.zeros((8, 128), F32)
    column = lanes() % 32
    mixed = []
    for k in range(4):
        x = padded[128 * (k + 1) : 128 * (k + 2), :]
        behind = pltpu.roll(padded[128 * k : 128 * (k + 1), :], 97, 1)
        ahead = pltpu.roll(padded[128 * (k + 2) : 128 * (k + 3), :], 31, 1)
        before = jnp.where(column == 0, behind, pltpu.roll(x, 1, 1))
        after = jnp.where(column == 31, ahead, pltpu.roll(x, 127, 1))
        curvature = before + after - 2.0 * x
        mixed.append(x + turn(curvature) * strength[128 * k : 128 * (k + 1), :])
    return [x + b for x, b in zip(mixed, right_product(right_ref, mixed))]


def correct_y(padded, mixed, target, strength, left_ref):
    line = lax.broadcasted_iota(jnp.int32, (128, 128), 0) % 8
    for i in range(4):
        for h in range(2):

            def near(half, offset):
                return padded[half, 8 + offset + 128 * i : 136 + offset + 128 * i, :]

            x = near(h, 0)
            before = jnp.where(line == 0, near(1 - h, 7 if h else -1), near(h, -1))
            after = jnp.where(line == 7, near(1 - h, 1 if h else -7), near(h, 1))
            curvature = before + after - 2.0 * x
            r = slice(128 * i, 128 * i + 128)
            mixed[h, r, :] = x + turn(curvature) * strength[h, r, :]

    def step(i, carry):
        rows = [at(256 * i + 64 * k, 64, 64) for k in range(4)]
        blocks = [jnp.concatenate([mixed[0, r, :], mixed[1, r, :]], 0) for r in rows]
        added = in_blocks(product(left_ref[...], left_operand(blocks, 1)))
        for x, b, r in zip(blocks, added, rows):
            value = x + b
            target[0, r, :] = value[0:64]
            target[1, r, :] = value[64:128]
        return carry

    lax.fori_loop(0, 2, step, 0)


def by_halves(matrix):
    low = [matrix[16 * s : 16 * s + 8] for s in range(8)]
    high = [matrix[16 * s + 8 : 16 * s + 16] for s in range(8)]
    return jnp.concatenate(low + high, 0)


def build_blocks(bx_ref, by_ref, right_ref, left_ref):
    for k in range(2):
        high, low = halves(by_halves(by_halves(by_ref[0, k]).T).T)
        for place, value in ((k, high), (2 + k, high), (4 + k, low)):
            left_ref[:, 128 * place : 128 * (place + 1)] = value
    real, imag = bx_ref[0, 0].T, bx_ref[0, 1].T
    zero = jnp.zeros_like(real)
    for c in range(2):
        pair = (real, imag) if c == 0 else (-imag, real)
        for field in range(2):
            blocks = [zero] * 4
            blocks[field], blocks[2 + field] = pair
            for quarter in range(4):
                high, low = halves(regroup(blocks, quarter))
                columns = slice(128 * quarter, 128 * (quarter + 1))
                for q in range(4):
                    base = 128 * q + 64 * c + 32 * field
                    for offset, value in ((0, high), (512, low), (1024, high)):
                        right_ref[offset + base : offset + base + 32, columns] = value[32 * q : 32 * q + 32]


def kernel(
    refv_ref,
    freq_ref,
    wave_hbm,
    vel_hbm,
    bx_hbm,
    by_hbm,
    left_x_hbm,
    twist_x_hbm,
    right_x_hbm,
    left_y_hbm,
    twist_y_hbm,
    out_ref,
    image_ref,
    wave_ref,
    vel_ref,
    bx_ref,
    by_ref,
    left_x,
    twist_x,
    right_x,
    left_y,
    twist_y,
    sent,
    got,
    work_a,
    work_b,
    operands,
    padded_x,
    padded_y,
    block_right,
    block_left,
    phase_real,
    phase_imag,
    turn_real,
    turn_imag,
    strength_x,
    strength_y,
    vel_all,
    vel_sent,
    vel_got,
    img_sent,
    img_got,
    part,
    shares,
    summed,
    totals,
    send_sem,
    recv_sem,
    small_send,
    small_recv,
    freq_send,
    freq_recv,
    load_sem,
):
    group = lax.axis_index("freq")
    me = lax.axis_index("slab")

    loads = []
    pairs = (
        (wave_hbm, wave_ref),
        (left_x_hbm, left_x),
        (twist_x_hbm, twist_x),
        (right_x_hbm, right_x.at[0:1024, :]),
        (vel_hbm, vel_ref),
        (left_y_hbm, left_y),
        (twist_y_hbm, twist_y),
        (bx_hbm, bx_ref),
        (by_hbm, by_ref),
    )
    for k, (source, target) in enumerate(pairs):
        loads.append(pltpu.make_async_copy(source, target, load_sem.at[k]))
        loads[-1].start()

    barrier = pltpu.get_barrier_semaphore()

    def greet_slab(i, carry):
        pl.semaphore_signal(barrier, inc=1, device_id=(group, lax.rem(me + i, SLABS)), device_id_type=MESH)
        return carry

    def greet_freq(i, carry):
        pl.semaphore_signal(barrier, inc=1, device_id=(lax.rem(group + i, GROUPS), me), device_id_type=MESH)
        return carry

    lax.fori_loop(1, GROUPS, greet_freq, 0)
    lax.fori_loop(1, SLABS, greet_slab, 0)

    def exchange(source, landing, send, recv):
        own = at(me * HALF, HALF, HALF)

        def step(i, carry):
            other = lax.rem(me + i * STRIDE, SLABS)
            pltpu.make_async_remote_copy(
                src_ref=source.at[at(other * HALF, HALF, HALF), :],
                dst_ref=landing.at[own, :],
                send_sem=send,
                recv_sem=recv,
                device_id=(group, other),
                device_id_type=MESH,
            ).start()
            return carry

        lax.fori_loop(1, SLABS, step, 0)
        pltpu.make_async_copy(source.at[own, :], landing.at[own, :], recv).start()

    def arrived(landing, recv):
        pltpu.make_async_copy(landing, landing, recv).wait()

    def left_here(source, send):
        count = HALF * (SLABS - 1)
        pltpu.make_async_copy(source.at[0:count, :], source.at[0:count, :], send).wait()

    def share(piece, landing, send, recv):
        def step(i, carry):
            other = lax.rem(group + i, GROUPS)
            pltpu.make_async_remote_copy(
                src_ref=piece(other),
                dst_ref=landing.at[group],
                send_sem=send,
                recv_sem=recv,
                device_id=(other, me),
                device_id_type=MESH,
            ).start()
            return carry

        lax.fori_loop(1, GROUPS, step, 0)
        pltpu.make_async_copy(piece(group), landing.at[group], recv).start()

    def shared_left(landing, send):
        pltpu.make_async_copy(landing.at[0 : GROUPS - 1], landing.at[0 : GROUPS - 1], send).wait()

    def field_out(k, h):
        exchange(sent.at[k, h], got.at[k, h], send_sem.at[k, h], recv_sem.at[k, h])

    def field_in(k, h):
        arrived(got.at[k, h], recv_sem.at[k, h])

    def both(step):
        def run(h, carry):
            step(h)
            return carry

        lax.fori_loop(0, 2, run, 0)

    loads[0].wait()
    loads[1].wait()
    loads[2].wait()

    def start_x(h):
        lines = at(8 * h, 8, 8)
        natural = []
        for g in range(4):
            pieces = [wave_ref[0, g % 2, g // 2, lines, 128 * a : 128 * (a + 1)] for a in range(16)]
            natural.append(jnp.concatenate(pieces, 0))
        put(work_a.at[h], outer_x([regroup(natural, q) for q in range(4)], left_x, twist_x, 1))

    both(start_x)
    loads[3].wait()
    loads[4].wait()

    def repeat_table(i, carry):
        right_x[at(1024 + 128 * i, 128, 128), :] = right_x[at(128 * i, 128, 128), :]
        return carry

    lax.fori_loop(0, 4, repeat_table, 0)
    pl.semaphore_wait(barrier, SLABS - 1 + GROUPS - 1)

    def send_x(h):
        put(sent.at[0, h], right_product(right_x, quarters(work_a.at[h])))
        field_out(0, h)

    both(send_x)
    share(lambda g: vel_ref, vel_all, freq_send.at[0], freq_recv.at[0])

    angular = jnp.full((1, 128), freq_ref[0], F32) * (2.0 * math.pi)
    speeds = [jnp.full((1, 128), refv_ref[d], F32) for d in range(2)]
    squares = [(angular / v) * (angular / v) for v in speeds]

    def positions_y(h, row, column):
        index_x = lax.rem(me, 16) + 16 * (lax.div(me, 16) * 32 + column)
        rest = row % 128
        return index_x, row // 128 + 4 * (16 * (rest // 8) + 8 * h + rest % 8)

    phase_factors(phase_real.at[0], phase_imag.at[0], squares[0], positions_y)
    loads[5].wait()
    loads[6].wait()

    def part_in(k, h, source, direction):
        operand = left_operand(quarters(source), direction)
        return in_blocks(product(left_y[h], operand))

    def accumulate(parts, h):
        for k, x in enumerate(parts):
            for m in range(2):
                r = slice(128 * k, 128 * (k + 1))
                value = x[128 * m : 128 * (m + 1)]
                work_b[m, r, :] = value if h == 0 else work_b[m, r, :] + value

    def products_y(h):
        rows = at(128 * h, 128, 128)
        total = product(left_y[0, rows, :], operands[0]) + product(left_y[1, rows, :], operands[1])
        return in_blocks(total)

    for h in range(2):
        field_in(0, h)
        butterfly_forward(got.at[0, h], work_a.at[h], twist_y, h)
        accumulate(part_in(0, h, work_a.at[h], 1), h)

    def shift_y(m):
        blocks = [
            rotated(b, phase_real[0, m, 128 * k : 128 * (k + 1), :], phase_imag[0, m, 128 * k : 128 * (k + 1), :])
            for k, b in enumerate(quarters(work_b.at[m]))
        ]
        operands[m] = left_operand(blocks, -1)

    both(shift_y)

    def back_y(h):
        put(work_a.at[h], products_y(h))
        butterfly_inverse(work_a.at[h], sent.at[1, h], twist_y, h, lambda x, r: x)
        field_out(1, h)

    both(back_y)

    arrived(vel_all, freq_recv.at[0])

    def pack_speed(f, carry):
        for low in range(2):
            a = 2 * f + low
            window = slice(128 * low, 128 * (low + 1))
            for d in range(2):
                x = vel_all[f, d, :, window]
                for q in range(4):
                    r = at(q * 128 + a * 8, 8, 8)
                    speed = spread(x, q)
                    strength = strength_of(speed, speeds[d])
                    for h in range(2):
                        strength_x[d, h, r, :] = strength[8 * h : 8 * h + 8]
                    if d == 0:
                        real, imag = split_factors(speed, speeds[d], angular)
                        for h in range(2):
                            turn_real[0, h, r, :] = real[8 * h : 8 * h + 8]
                            turn_imag[0, h, r, :] = imag[8 * h : 8 * h + 8]
            blocks = [vel_all[f, g % 2, 8 * (g // 2) : 8 * (g // 2) + 8, window] for g in range(4)]
            for q in range(4):
                vel_sent[at((q * 16 + a) * 8, 8, 8), :] = regroup(blocks, q)
        return carry

    lax.fori_loop(0, GROUPS, pack_speed, 0)
    exchange(vel_sent, vel_got, small_send.at[0], small_recv.at[0])
    loads[7].wait()
    loads[8].wait()
    build_blocks(bx_ref, by_ref, block_right, block_left)

    def correct_lines(h):
        field_in(1, h)
        blocks = inverse_inner_x(quarters(got.at[1, h]), right_x)
        blocks = outer_x(blocks, left_x, twist_x, -1)
        blocks = [
            rotated(b, turn_real[0, h, 128 * k : 128 * (k + 1), :], turn_imag[0, h, 128 * k : 128 * (k + 1), :])
            for k, b in enumerate(blocks)
        ]
        put(sent.at[2, h], correct_x(blocks, padded_x, strength_x.at[0, h], block_right))
        field_out(2, h)

    both(correct_lines)

    arrived(vel_got, small_recv.at[0])

    def unpack_speed(i, carry):
        r = at(64 * i, 64, 64)
        x = vel_got[r, :]
        for d in range(2):
            for h in range(2):
                speed = spread(x, 2 * h + d)
                strength_y[d, h, r, :] = strength_of(speed, speeds[d])
                if d == 1:
                    real, imag = split_factors(speed, speeds[d], angular)
                    turn_real[1, h, r, :] = real
                    turn_imag[1, h, r, :] = imag
        return carry

    lax.fori_loop(0, 8, unpack_speed, 0)

    zeros = jnp.zeros((8, 128), F32)
    for h in range(2):
        padded_y[h, 0:8, :] = zeros
        padded_y[h, 520:528, :] = zeros

    def positions_x(h, row, column):
        line = me * 16 + 8 * h + row % 8
        index_x = row // 8 % 16 + 16 * (row // 128 * 32 + column)
        return index_x, line // 256 + 4 * (line % 256)

    phase_factors(phase_real.at[1], phase_imag.at[1], squares[1], positions_x)

    def fill_y(h):
        field_in(2, h)
        padded_y[h, 8:520, :] = got[2, h]

    both(fill_y)
    correct_y(padded_y, work_a, work_b, strength_y.at[0], block_left)

    def start_y(h):
        butterfly_forward(work_b.at[h], work_a.at[h], twist_y, h)
        operands[h] = left_operand(quarters(work_a.at[h]), 1)

    both(start_y)

    def send_y(h):
        put(sent.at[3, h], products_y(h))
        field_out(3, h)

    both(send_y)

    def image_y(i, carry):
        group_of = lanes() // 32
        r = at(64 * i, 64, 64)
        pieces = []
        for h in range(2):
            x = work_b[h, r, :]
            value = x * pltpu.roll(x, 96, 1)
            pieces.append(value - pltpu.roll(value, 64, 1))
        packed = jnp.where(group_of == 1, pltpu.roll(pieces[1], 32, 1), 0.0)
        img_sent[r, :] = jnp.where(group_of == 0, pieces[0], packed)
        return carry

    lax.fori_loop(0, 8, image_y, 0)
    exchange(img_sent, img_got, small_send.at[1], small_recv.at[1])

    def shift_x(h):
        field_in(3, h)
        blocks = outer_x(quarters(got.at[3, h]), left_x, twist_x, 1)
        blocks = right_product(right_x, blocks)
        blocks = [
            rotated(b, phase_real[1, h, 128 * k : 128 * (k + 1), :], phase_imag[1, h, 128 * k : 128 * (k + 1), :])
            for k, b in enumerate(blocks)
        ]
        blocks = inverse_inner_x(blocks, right_x)
        put(sent.at[4, h], outer_x(blocks, left_x, twist_x, -1))
        field_out(4, h)

    both(shift_x)

    def reduce_out(d):
        share(lambda g: part.at[d, at(2 * g, 2, 2)], shares.at[d], freq_send.at[1 + d], freq_recv.at[1 + d])

    def gather_out(d):
        arrived(shares.at[d], freq_recv.at[1 + d])
        total = shares[d, 0]
        for g in range(1, GROUPS):
            total = total + shares[d, g]
        summed[d] = total
        share(lambda g: summed.at[d], totals.at[d], freq_send.at[3 + d], freq_recv.at[3 + d])

    arrived(img_got, small_recv.at[1])

    def image_x(i, carry):
        group_of = lanes() // 32
        for low in range(2):
            a = 2 * i + low
            for h in range(2):
                result = jnp.zeros((8, 128), F32)
                for q in range(4):
                    x = img_got[at((q * 16 + a) * 8, 8, 8), :]
                    amount = 32 * (q - h) % 128
                    result = jnp.where(group_of == q, pltpu.roll(x, amount, 1) if amount else x, result)
                part[0, a, 8 * h : 8 * h + 8, :] = result
        return carry

    lax.fori_loop(0, 8, image_x, 0)
    reduce_out(0)

    for h in range(2):
        field_in(4, h)
        accumulate(part_in(4, h, got.at[4, h], -1), h)

    def finish_y(h):
        def split_y(x, r):
            return rotated(x, turn_real[1, h, r, :], turn_imag[1, h, r, :])

        butterfly_inverse(work_b.at[h], work_a.at[h], twist_y, h, split_y)
        padded_y[h, 8:520, :] = work_a[h]

    both(finish_y)
    correct_y(padded_y, work_a, sent.at[5], strength_y.at[1], block_left)

    def last_out(h):
        field_out(5, h)

    both(last_out)
    gather_out(0)

    def last_lines(h):
        field_in(5, h)
        blocks = correct_x(quarters(got.at[5, h]), padded_x, strength_x.at[1, h], block_right)
        whole = [regroup(blocks, g) for g in range(4)]
        image = whole[0] * whole[1] - whole[2] * whole[3]
        lines = at(8 * h, 8, 8)
        for a in range(16):
            r = slice(8 * a, 8 * a + 8)
            part[1, a, lines, :] = image[r]
            for g in range(4):
                out_ref[0, g % 2, g // 2, lines, 128 * a : 128 * (a + 1)] = whole[g][r]

    both(last_lines)
    reduce_out(1)
    gather_out(1)

    for d in range(2):
        arrived(totals.at[d], freq_recv.at[3 + d])
        for a in range(16):
            image_ref[d, :, 128 * a : 128 * (a + 1)] = totals[d, a // 2, a % 2]

    for k in range(6):
        for h in range(2):
            left_here(sent.at[k, h], send_sem.at[k, h])
    left_here(vel_sent, small_send.at[0])
    left_here(img_sent, small_send.at[1])
    shared_left(vel_all, freq_send.at[0])
    for d in range(2):
        shared_left(shares.at[d], freq_send.at[1 + d])
        shared_left(totals.at[d], freq_send.at[3 + d])


def scratch():
    def vmem(*shape, dtype=F32):
        return pltpu.VMEM(shape, dtype)

    def dma(*shape):
        return pltpu.SemaphoreType.DMA(shape)

    state = (2, 512, 128)
    return [
        vmem(1, 2, 2, 16, NX),
        vmem(2, 16, 256),
        vmem(1, 2, 128, 128),
        vmem(1, 2, 128, 128),
        vmem(128, 768, dtype=BF16),
        vmem(2, 512, 128),
        vmem(1536, 512, dtype=BF16),
        vmem(2, 256, 768, dtype=BF16),
        vmem(2, 2, 512, 128),
        vmem(6, *state),
        vmem(6, *state),
        vmem(*state),
        vmem(*state),
        vmem(2, 768, 512, dtype=BF16),
        vmem(768, 128),
        vmem(2, 528, 128),
        vmem(1536, 512, dtype=BF16),
        vmem(128, 768, dtype=BF16),
        vmem(2, *state),
        vmem(2, *state),
        vmem(2, *state),
        vmem(2, *state),
        vmem(2, *state),
        vmem(2, *state),
        vmem(GROUPS, 2, 16, 256),
        vmem(512, 128),
        vmem(512, 128),
        vmem(512, 128),
        vmem(512, 128),
        vmem(2, 16, 16, 128),
        vmem(2, GROUPS, 2, 16, 128),
        vmem(2, 2, 16, 128),
        vmem(2, GROUPS, 2, 16, 128),
        dma(6, 2),
        dma(6, 2),
        dma(2),
        dma(2),
        dma(5),
        dma(5),
        dma(9),
    ]


def body(wavefield, velocity, reference_velocity, frequencies, block_x, block_y):
    vmem, smem = pl.BlockSpec(memory_space=pltpu.VMEM), pl.BlockSpec(memory_space=pltpu.SMEM)
    anywhere = pl.BlockSpec(memory_space=pl.ANY)
    constants = [jnp.asarray(t) for t in tables()]
    call = pl.pallas_call(
        kernel,
        out_shape=(
            jax.ShapeDtypeStruct(wavefield.shape, F32),
            jax.ShapeDtypeStruct((2, 16, NX), F32),
        ),
        in_specs=[smem, smem] + [anywhere] * (4 + len(constants)),
        out_specs=(vmem, vmem),
        scratch_shapes=scratch(),
        compiler_params=pltpu.CompilerParams(
            collective_id=0, has_side_effects=True, vmem_limit_bytes=60 * 1024 * 1024
        ),
    )
    return call(reference_velocity, frequencies, wavefield, velocity, block_x, block_y, *constants)


def solution(mesh):
    in_specs = (
        P("freq", None, None, "slab", None),
        P(None, "slab", "freq"),
        P(),
        P("freq"),
        P("freq", None, None, None),
        P("freq", None, None, None),
    )
    out_specs = (P("freq", None, None, "slab", None), P(None, "slab", None))
    return jax.shard_map(body, mesh=mesh, in_specs=in_specs, out_specs=out_specs, check_vma=False)
```

```python
import functools
import math

import jax
import jax.numpy as jnp
import numpy as np
from jax import lax
from jax.experimental import pallas as pl
from jax.experimental.pallas import tpu as pltpu
from jax.sharding import PartitionSpec as P

F32 = jnp.float32
BF16 = jnp.bfloat16
MESH = pl.DeviceIdType.MESH

NX = 2048
NY = 1024
SLABS = 64
GROUPS = 8
HALF = 8
STRIDE = 27
spacing = 12.5
depth_step = 10.0


def split_table(table):
    high = table.astype(jnp.bfloat16)
    low = (table - high.astype(np.float64)).astype(jnp.bfloat16)
    return high, low


def angle(product, period):
    turns = 2.0 * math.pi * (product % period) / period
    return np.cos(turns), -np.sin(turns)


@functools.lru_cache(maxsize=None)
def tables():
    sixteen = np.arange(16)
    cos, sin = angle(sixteen[:, None] * sixteen[None, :], 16)
    eye = np.eye(HALF)
    high, low = split_table(np.concatenate([np.kron(cos, eye), np.kron(sin, eye)], 1))
    left_x = np.concatenate([high, high, low], 1)
    place = np.arange(16)[:, None] * 16 + np.arange(8)[None, :]
    places = [(place + 8 * h).reshape(128) for h in range(2)]
    order = np.concatenate(places)
    left_y = []
    for h in range(2):
        high, low = split_table(np.concatenate(angle(order[:, None] * places[h][None, :], 256), 1))
        left_y.append(np.concatenate([high, high, low], 1))
    left_y = np.stack(left_y)
    inner = np.arange(128)
    cos, sin = angle(inner[:, None] * inner[None, :], 128)
    full = np.zeros((2, 2, 2, 32, 2, 2, 2, 32))
    for c, d, block in ((0, 0, cos), (0, 1, sin), (1, 0, -sin), (1, 1, cos)):
        full[:, c, :, :, :, d, :, :] = block.reshape(2, 2, 32, 2, 2, 32)
    high, low = split_table(full.reshape(256, 256))
    right_x = np.concatenate([high, low, high], 0)
    quarter, outer, column = np.arange(4), np.arange(16), np.arange(32)
    position = quarter[:, None] * 32 + column[None, :]
    product = outer[None, :, None] * position[:, None, :]
    twist_x = []
    for part in angle(product, NX):
        part = np.broadcast_to(part[:, :, None, None, :], (4, 16, HALF, 4, 32))
        twist_x.append(part.reshape(512, 128))
    product = np.arange(4)[None, :, None] * np.stack(places)[:, None, :]
    twist_y = []
    for part in angle(product, NY):
        part = np.broadcast_to(part.reshape(2, 512, 1), (2, 512, 128))
        twist_y.append(part)
    return left_x, np.stack(twist_x).astype(np.float32), right_x, left_y, np.stack(twist_y).astype(np.float32)


def lanes(rows=1):
    return lax.broadcasted_iota(jnp.int32, (rows, 128), 1)


def turn(x):
    sign = jnp.where(lanes() < 64, -1.0, 1.0)
    return pltpu.roll(x, 64, 1) * sign


def unturn(x):
    sign = jnp.where(lanes() < 64, 1.0, -1.0)
    return pltpu.roll(x, 64, 1) * sign


def conjugate(x):
    return x * jnp.where(lanes() < 64, 1.0, -1.0)


def halves(x):
    high = x.astype(BF16)
    return high, (x - high.astype(F32)).astype(BF16)


def left_operand(blocks, direction):
    columns = []
    for x in blocks:
        y = turn(x) if direction > 0 else unturn(x)
        high_x, low_x = halves(x)
        high_y, low_y = halves(y)
        columns.append(jnp.concatenate([high_x, high_y, low_x, low_y, high_x, high_y], 0))
    return jnp.concatenate(columns, 1)


def product(left, right):
    return jnp.dot(left, right, preferred_element_type=F32)


def in_blocks(total):
    return [total[:, 128 * k : 128 * (k + 1)] for k in range(total.shape[1] // 128)]


def right_product(table_ref, blocks):
    odd = lanes() // 32 % 2 == 1
    rows = blocks[0].shape[0]
    operand = []
    for p in range(2):
        x, y = blocks[2 * p], blocks[2 * p + 1]
        first = jnp.where(odd, pltpu.roll(y, 32, 1), x)
        second = jnp.where(odd, y, pltpu.roll(x, 96, 1))
        operand.append(halves(jnp.concatenate([first, second], 0)))
    (high_0, low_0), (high_1, low_1) = operand
    total = product(jnp.concatenate([high_0, high_1, high_0, high_1, low_0, low_1], 1), table_ref[...])
    results = []
    for p in range(2):
        first = total[:rows, 128 * p : 128 * (p + 1)]
        second = total[rows:, 128 * p : 128 * (p + 1)]
        results.append(jnp.where(odd, pltpu.roll(second, 32, 1), first))
        results.append(jnp.where(odd, second, pltpu.roll(first, 96, 1)))
    return results


def rotated(x, factor_real, factor_imag):
    return x * factor_real + turn(x) * factor_imag


def rotated_back(x, factor_real, factor_imag):
    return x * factor_real + unturn(x) * factor_imag


def at(start, size, unit):
    return pl.ds(pl.multiple_of(start, unit), size)


def quarters(ref):
    return [ref[128 * k : 128 * (k + 1), :] for k in range(4)]


def put(ref, blocks):
    for k, x in enumerate(blocks):
        ref[128 * k : 128 * (k + 1), :] = x


def outer_x(blocks, left_ref, twist, direction):
    rows = [slice(128 * k, 128 * (k + 1)) for k in range(4)]
    if direction < 0:
        blocks = [rotated_back(b, twist[0, r, :], twist[1, r, :]) for b, r in zip(blocks, rows)]
    blocks = in_blocks(product(left_ref[...], left_operand(blocks, direction)))
    if direction > 0:
        blocks = [rotated(b, twist[0, r, :], twist[1, r, :]) for b, r in zip(blocks, rows)]
    return blocks


def inverse_inner_x(blocks, right_ref):
    return [conjugate(b) for b in right_product(right_ref, [conjugate(b) for b in blocks])]


def butterfly_forward(source, target, twist, h):
    for i in range(4):
        rows = [slice(128 * k + 32 * i, 128 * k + 32 * i + 32) for k in range(4)]
        x0, x1, x2, x3 = [source[r, :] for r in rows]
        even, odd = x0 + x2, x1 + x3
        minus, spun = x0 - x2, turn(x1 - x3)
        results = [even + odd, minus - spun, even - odd, minus + spun]
        for k, r in enumerate(rows):
            value = results[k]
            if k > 0:
                value = rotated(value, twist[0, h, r, :], twist[1, h, r, :])
            target[r, :] = value


def butterfly_inverse(source, target, twist, h, finish):
    for i in range(4):
        rows = [slice(128 * k + 32 * i, 128 * k + 32 * i + 32) for k in range(4)]
        x0, x1, x2, x3 = [source[r, :] for r in rows]
        x1, x2, x3 = [
            rotated_back(x, twist[0, h, r, :], twist[1, h, r, :])
            for x, r in zip((x1, x2, x3), rows[1:])
        ]
        even, odd = x0 + x2, x1 + x3
        minus, spun = x0 - x2, turn(x1 - x3)
        results = [even + odd, minus + spun, even - odd, minus - spun]
        for value, r in zip(results, rows):
            target[r, :] = finish(value, r)


def series(square, first):
    value = jnp.full_like(square, 1.0 / math.factorial(16 + first))
    for n in range(7, -1, -1):
        value = value * square + (-1.0) ** n / math.factorial(2 * n + first)
    return value


def wavenumber(index, length):
    signed = jnp.where(index >= length // 2, index - length, index)
    return signed.astype(F32) * (2.0 * math.pi / (length * spacing))


def phase_factors(target_real, target_imag, ratio_square, positions):
    def step(i, carry):
        r = at(64 * lax.rem(i, 8), 64, 64)
        h = lax.div(i, 8)
        row = lax.broadcasted_iota(jnp.int32, (64, 128), 0) + 64 * lax.rem(i, 8)
        column = lanes(64) % 32
        index_x, index_y = positions(h, row, column)
        wave_x, wave_y = wavenumber(index_x, NX), wavenumber(index_y, NY)
        vertical = ratio_square - wave_x * wave_x - wave_y * wave_y
        square = jnp.abs(vertical) * (depth_step * depth_step)
        size = jnp.sqrt(square)
        travels = vertical >= 0
        scale = 1.0 / (NX * NY)
        target_real[h, r, :] = jnp.where(travels, series(square, 0), jnp.exp(-size)) * scale
        target_imag[h, r, :] = jnp.where(travels, size * series(square, 1), 0.0) * scale
        return carry

    lax.fori_loop(0, 16, step, 0)


def split_factors(speed, ref_speed, angular):
    turned = angular * depth_step * (1.0 / speed - 1.0 / ref_speed)
    square = turned * turned
    return series(square, 0), turned * series(square, 1)


def strength_of(speed, ref_speed):
    return 0.5 * (1.0 - ref_speed / speed)


def spread(x, group):
    x = jnp.where(lanes() // 32 == group, x, 0.0)
    x = x + pltpu.roll(x, 64, 1)
    return x + pltpu.roll(x, 32, 1)


def regroup(blocks, index):
    group = lanes() // 32
    result = jnp.zeros_like(blocks[0])
    for g, x in enumerate(blocks):
        shift = 32 * (g - index) % 128
        result = jnp.where(group == g, pltpu.roll(x, shift, 1) if shift else x, result)
    return result


def correct_x(blocks, padded, strength, right_ref):
    for k in range(4):
        padded[128 * (k + 1) : 128 * (k + 2), :] = blocks[k]
    padded[0:8, :] = jnp.zeros((8, 128), F32)
    padded[8:128, :] = blocks[3][0:120]
    padded[640:760, :] = blocks[0][8:128]
    padded[760:768, :] = jnp.zeros((8, 128), F32)
    column = lanes() % 32
    mixed = []
    for k in range(4):
        x = padded[128 * (k + 1) : 128 * (k + 2), :]
        behind = pltpu.roll(padded[128 * k : 128 * (k + 1), :], 97, 1)
        ahead = pltpu.roll(padded[128 * (k + 2) : 128 * (k + 3), :], 31, 1)
        before = jnp.where(column == 0, behind, pltpu.roll(x, 1, 1))
        after = jnp.where(column == 31, ahead, pltpu.roll(x, 127, 1))
        curvature = before + after - 2.0 * x
        mixed.append(x + turn(curvature) * strength[128 * k : 128 * (k + 1), :])
    return [x + b for x, b in zip(mixed, right_product(right_ref, mixed))]


def correct_y(padded, mixed, target, strength, left_ref):
    line = lax.broadcasted_iota(jnp.int32, (128, 128), 0) % 8
    for i in range(4):
        for h in range(2):

            def near(half, offset):
                return padded[half, 8 + offset + 128 * i : 136 + offset + 128 * i, :]

            x = near(h, 0)
            before = jnp.where(line == 0, near(1 - h, 7 if h else -1), near(h, -1))
            after = jnp.where(line == 7, near(1 - h, 1 if h else -7), near(h, 1))
            curvature = before + after - 2.0 * x
            r = slice(128 * i, 128 * i + 128)
            mixed[h, r, :] = x + turn(curvature) * strength[h, r, :]

    def step(i, carry):
        rows = [at(256 * i + 64 * k, 64, 64) for k in range(4)]
        blocks = [jnp.concatenate([mixed[0, r, :], mixed[1, r, :]], 0) for r in rows]
        added = in_blocks(product(left_ref[...], left_operand(blocks, 1)))
        for x, b, r in zip(blocks, added, rows):
            value = x + b
            target[0, r, :] = value[0:64]
            target[1, r, :] = value[64:128]
        return carry

    lax.fori_loop(0, 2, step, 0)


def by_halves(matrix):
    low = [matrix[16 * s : 16 * s + 8] for s in range(8)]
    high = [matrix[16 * s + 8 : 16 * s + 16] for s in range(8)]
    return jnp.concatenate(low + high, 0)


def build_blocks(bx_ref, by_ref, right_ref, left_ref):
    for k in range(2):
        high, low = halves(by_halves(by_halves(by_ref[0, k]).T).T)
        for place, value in ((k, high), (2 + k, high), (4 + k, low)):
            left_ref[:, 128 * place : 128 * (place + 1)] = value
    real, imag = bx_ref[0, 0].T, bx_ref[0, 1].T
    front = lanes() < 64
    for c in range(2):
        x, y = (real, imag) if c == 0 else (-imag, real)
        pairs = (jnp.where(front, x, pltpu.roll(y, 64, 1)), jnp.where(front, pltpu.roll(x, 64, 1), y))
        for p, pair in enumerate(pairs):
            high, low = halves(pair)
            columns = slice(128 * p, 128 * (p + 1))
            for q in range(4):
                base = 128 * (q // 2) + 64 * c + 32 * (q % 2)
                for offset, value in ((0, high), (256, low), (512, high)):
                    right_ref[offset + base : offset + base + 32, columns] = value[32 * q : 32 * q + 32]


def kernel(
    refv_ref,
    freq_ref,
    wave_hbm,
    vel_hbm,
    bx_hbm,
    by_hbm,
    left_x_hbm,
    twist_x_hbm,
    right_x_hbm,
    left_y_hbm,
    twist_y_hbm,
    out_ref,
    image_ref,
    wave_ref,
    vel_ref,
    bx_ref,
    by_ref,
    left_x,
    twist_x,
    right_x,
    left_y,
    twist_y,
    sent,
    got,
    work_a,
    work_b,
    operands,
    padded_x,
    padded_y,
    block_right,
    block_left,
    phase_real,
    phase_imag,
    turn_real,
    turn_imag,
    strength_x,
    strength_y,
    vel_all,
    vel_sent,
    vel_got,
    img_sent,
    img_got,
    part,
    shares,
    summed,
    totals,
    send_sem,
    recv_sem,
    small_send,
    small_recv,
    freq_send,
    freq_recv,
    load_sem,
):
    group = lax.axis_index("freq")
    me = lax.axis_index("slab")

    loads = []
    pairs = (
        (wave_hbm, wave_ref),
        (left_x_hbm, left_x),
        (twist_x_hbm, twist_x),
        (right_x_hbm, right_x),
        (vel_hbm, vel_ref),
        (left_y_hbm, left_y),
        (twist_y_hbm, twist_y),
        (bx_hbm, bx_ref),
        (by_hbm, by_ref),
    )
    for k, (source, target) in enumerate(pairs):
        loads.append(pltpu.make_async_copy(source, target, load_sem.at[k]))
        loads[-1].start()

    barrier = pltpu.get_barrier_semaphore()

    def greet_slab(i, carry):
        pl.semaphore_signal(barrier, inc=1, device_id=(group, lax.rem(me + i, SLABS)), device_id_type=MESH)
        return carry

    def greet_freq(i, carry):
        pl.semaphore_signal(barrier, inc=1, device_id=(lax.rem(group + i, GROUPS), me), device_id_type=MESH)
        return carry

    lax.fori_loop(1, GROUPS, greet_freq, 0)
    lax.fori_loop(1, SLABS, greet_slab, 0)

    def exchange(source, landing, send, recv):
        own = at(me * HALF, HALF, HALF)

        def step(i, carry):
            for k in range(1, 4):
                other = lax.rem(me + (3 * i + k) * STRIDE, SLABS)
                pltpu.make_async_remote_copy(
                    src_ref=source.at[at(other * HALF, HALF, HALF), :],
                    dst_ref=landing.at[own, :],
                    send_sem=send,
                    recv_sem=recv,
                    device_id=(group, other),
                    device_id_type=MESH,
                ).start()
            return carry

        lax.fori_loop(0, (SLABS - 1) // 3, step, 0)
        pltpu.make_async_copy(source.at[own, :], landing.at[own, :], recv).start()

    def arrived(landing, recv):
        pltpu.make_async_copy(landing, landing, recv).wait()

    def left_here(source, send):
        count = HALF * (SLABS - 1)
        pltpu.make_async_copy(source.at[0:count, :], source.at[0:count, :], send).wait()

    def share(piece, landing, send, recv):
        def step(i, carry):
            other = lax.rem(group + i, GROUPS)
            pltpu.make_async_remote_copy(
                src_ref=piece(other),
                dst_ref=landing.at[group],
                send_sem=send,
                recv_sem=recv,
                device_id=(other, me),
                device_id_type=MESH,
            ).start()
            return carry

        lax.fori_loop(1, GROUPS, step, 0)
        pltpu.make_async_copy(piece(group), landing.at[group], recv).start()

    def shared_left(landing, send):
        pltpu.make_async_copy(landing.at[0 : GROUPS - 1], landing.at[0 : GROUPS - 1], send).wait()

    def field_out(k, h):
        exchange(sent.at[k, h], got.at[k, h], send_sem.at[k, h], recv_sem.at[k, h])

    def field_in(k, h):
        arrived(got.at[k, h], recv_sem.at[k, h])

    def both(step):
        def run(h, carry):
            step(h)
            return carry

        lax.fori_loop(0, 2, run, 0)

    loads[0].wait()
    loads[1].wait()
    loads[2].wait()

    def start_x(h):
        lines = at(8 * h, 8, 8)
        natural = []
        for g in range(4):
            pieces = [wave_ref[0, g % 2, g // 2, lines, 128 * a : 128 * (a + 1)] for a in range(16)]
            natural.append(jnp.concatenate(pieces, 0))
        put(work_a.at[h], outer_x([regroup(natural, q) for q in range(4)], left_x, twist_x, 1))

    both(start_x)
    loads[3].wait()
    loads[4].wait()

    pl.semaphore_wait(barrier, SLABS - 1 + GROUPS - 1)

    def send_x(h):
        put(sent.at[0, h], right_product(right_x, quarters(work_a.at[h])))
        field_out(0, h)

    share(lambda g: vel_ref, vel_all, freq_send.at[0], freq_recv.at[0])
    both(send_x)

    angular = jnp.full((1, 128), freq_ref[0], F32) * (2.0 * math.pi)
    speeds = [jnp.full((1, 128), refv_ref[d], F32) for d in range(2)]
    squares = [(angular / v) * (angular / v) for v in speeds]

    def positions_y(h, row, column):
        index_x = lax.rem(me, 16) + 16 * (lax.div(me, 16) * 32 + column)
        rest = row % 128
        return index_x, row // 128 + 4 * (16 * (rest // 8) + 8 * h + rest % 8)

    phase_factors(phase_real.at[0], phase_imag.at[0], squares[0], positions_y)

    arrived(vel_all, freq_recv.at[0])

    def pack_speed(f, carry):
        for low in range(2):
            a = 2 * f + low
            window = slice(128 * low, 128 * (low + 1))
            for d in range(2):
                x = vel_all[f, d, :, window]
                for q in range(4):
                    r = at(q * 128 + a * 8, 8, 8)
                    speed = spread(x, q)
                    strength = strength_of(speed, speeds[d])
                    for h in range(2):
                        strength_x[d, h, r, :] = strength[8 * h : 8 * h + 8]
                    if d == 0:
                        real, imag = split_factors(speed, speeds[d], angular)
                        for h in range(2):
                            turn_real[0, h, r, :] = real[8 * h : 8 * h + 8]
                            turn_imag[0, h, r, :] = imag[8 * h : 8 * h + 8]
            blocks = [vel_all[f, g % 2, 8 * (g // 2) : 8 * (g // 2) + 8, window] for g in range(4)]
            for q in range(4):
                vel_sent[at((q * 16 + a) * 8, 8, 8), :] = regroup(blocks, q)
        return carry

    lax.fori_loop(0, GROUPS, pack_speed, 0)
    exchange(vel_sent, vel_got, small_send.at[0], small_recv.at[0])
    loads[5].wait()
    loads[6].wait()

    def part_in(k, h, source, direction):
        operand = left_operand(quarters(source), direction)
        return in_blocks(product(left_y[h], operand))

    def accumulate(parts, h):
        for k, x in enumerate(parts):
            for m in range(2):
                r = slice(128 * k, 128 * (k + 1))
                value = x[128 * m : 128 * (m + 1)]
                work_b[m, r, :] = value if h == 0 else work_b[m, r, :] + value

    def products_y(h):
        rows = at(128 * h, 128, 128)
        total = product(left_y[0, rows, :], operands[0]) + product(left_y[1, rows, :], operands[1])
        return in_blocks(total)

    for h in range(2):
        field_in(0, h)
        butterfly_forward(got.at[0, h], work_a.at[h], twist_y, h)
        accumulate(part_in(0, h, work_a.at[h], 1), h)

    def shift_y(m):
        blocks = [
            rotated(b, phase_real[0, m, 128 * k : 128 * (k + 1), :], phase_imag[0, m, 128 * k : 128 * (k + 1), :])
            for k, b in enumerate(quarters(work_b.at[m]))
        ]
        operands[m] = left_operand(blocks, -1)

    both(shift_y)

    def back_y(h):
        put(work_a.at[h], products_y(h))
        butterfly_inverse(work_a.at[h], sent.at[1, h], twist_y, h, lambda x, r: x)
        field_out(1, h)

    both(back_y)

    loads[7].wait()
    loads[8].wait()
    build_blocks(bx_ref, by_ref, block_right, block_left)

    def correct_lines(h):
        field_in(1, h)
        blocks = inverse_inner_x(quarters(got.at[1, h]), right_x)
        blocks = outer_x(blocks, left_x, twist_x, -1)
        blocks = [
            rotated(b, turn_real[0, h, 128 * k : 128 * (k + 1), :], turn_imag[0, h, 128 * k : 128 * (k + 1), :])
            for k, b in enumerate(blocks)
        ]
        put(sent.at[2, h], correct_x(blocks, padded_x, strength_x.at[0, h], block_right))
        field_out(2, h)

    both(correct_lines)

    arrived(vel_got, small_recv.at[0])

    def unpack_speed(i, carry):
        r = at(64 * i, 64, 64)
        x = vel_got[r, :]
        for d in range(2):
            for h in range(2):
                speed = spread(x, 2 * h + d)
                strength_y[d, h, r, :] = strength_of(speed, speeds[d])
                if d == 1:
                    real, imag = split_factors(speed, speeds[d], angular)
                    turn_real[1, h, r, :] = real
                    turn_imag[1, h, r, :] = imag
        return carry

    lax.fori_loop(0, 8, unpack_speed, 0)

    zeros = jnp.zeros((8, 128), F32)
    for h in range(2):
        padded_y[h, 0:8, :] = zeros
        padded_y[h, 520:528, :] = zeros

    def positions_x(h, row, column):
        line = me * 16 + 8 * h + row % 8
        index_x = row // 8 % 16 + 16 * (row // 128 * 32 + column)
        return index_x, line // 256 + 4 * (line % 256)

    phase_factors(phase_real.at[1], phase_imag.at[1], squares[1], positions_x)

    def fill_y(h):
        field_in(2, h)
        padded_y[h, 8:520, :] = got[2, h]

    both(fill_y)
    correct_y(padded_y, work_a, work_b, strength_y.at[0], block_left)

    def start_y(h):
        butterfly_forward(work_b.at[h], work_a.at[h], twist_y, h)
        operands[h] = left_operand(quarters(work_a.at[h]), 1)

    both(start_y)

    def send_y(h):
        put(sent.at[3, h], products_y(h))
        field_out(3, h)

    both(send_y)

    def image_y(i, carry):
        group_of = lanes() // 32
        r = at(64 * i, 64, 64)
        pieces = []
        for h in range(2):
            x = work_b[h, r, :]
            value = x * pltpu.roll(x, 96, 1)
            pieces.append(value - pltpu.roll(value, 64, 1))
        packed = jnp.where(group_of == 1, pltpu.roll(pieces[1], 32, 1), 0.0)
        img_sent[r, :] = jnp.where(group_of == 0, pieces[0], packed)
        return carry

    lax.fori_loop(0, 8, image_y, 0)
    def shift_x(h):
        field_in(3, h)
        blocks = outer_x(quarters(got.at[3, h]), left_x, twist_x, 1)
        blocks = right_product(right_x, blocks)
        blocks = [
            rotated(b, phase_real[1, h, 128 * k : 128 * (k + 1), :], phase_imag[1, h, 128 * k : 128 * (k + 1), :])
            for k, b in enumerate(blocks)
        ]
        blocks = inverse_inner_x(blocks, right_x)
        put(sent.at[4, h], outer_x(blocks, left_x, twist_x, -1))
        field_out(4, h)

    both(shift_x)

    for h in range(2):
        field_in(4, h)
        accumulate(part_in(4, h, got.at[4, h], -1), h)
        if h == 0:
            exchange(img_sent, img_got, small_send.at[1], small_recv.at[1])

    def finish_y(h):
        def split_y(x, r):
            return rotated(x, turn_real[1, h, r, :], turn_imag[1, h, r, :])

        butterfly_inverse(work_b.at[h], work_a.at[h], twist_y, h, split_y)
        padded_y[h, 8:520, :] = work_a[h]

    both(finish_y)
    correct_y(padded_y, work_a, sent.at[5], strength_y.at[1], block_left)

    def last_out(h):
        field_out(5, h)

    both(last_out)

    def reduce_out(d, h):
        k = 1 + 2 * d + h
        share(lambda g: part.at[d, h, at(2 * g, 2, 2)], shares.at[d, h], freq_send.at[k], freq_recv.at[k])

    def gather_out(d, h):
        arrived(shares.at[d, h], freq_recv.at[1 + 2 * d + h])
        total = shares[d, h, 0]
        for g in range(1, GROUPS):
            total = total + shares[d, h, g]
        summed[d, h] = total
        k = 5 + 2 * d + h
        share(lambda g: summed.at[d, h], totals.at[d, h], freq_send.at[k], freq_recv.at[k])

    arrived(img_got, small_recv.at[1])

    def image_x(i, carry):
        group_of = lanes() // 32
        for low in range(2):
            a = 2 * i + low
            for h in range(2):
                result = jnp.zeros((8, 128), F32)
                for q in range(4):
                    x = img_got[at((q * 16 + a) * 8, 8, 8), :]
                    amount = 32 * (q - h) % 128
                    result = jnp.where(group_of == q, pltpu.roll(x, amount, 1) if amount else x, result)
                part[0, h, a] = result
        return carry

    lax.fori_loop(0, 8, image_x, 0)
    for h in range(2):
        reduce_out(0, h)

    def last_lines(h):
        field_in(5, h)
        blocks = correct_x(quarters(got.at[5, h]), padded_x, strength_x.at[1, h], block_right)
        whole = [regroup(blocks, g) for g in range(4)]
        image = whole[0] * whole[1] - whole[2] * whole[3]
        lines = slice(8 * h, 8 * h + 8)
        for a in range(16):
            part[1, h, a] = image[8 * a : 8 * a + 8]
        reduce_out(1, h)
        for a in range(16):
            for g in range(4):
                out_ref[0, g % 2, g // 2, lines, 128 * a : 128 * (a + 1)] = whole[g][8 * a : 8 * a + 8]

    last_lines(0)
    for h in range(2):
        gather_out(0, h)
    last_lines(1)
    for h in range(2):
        gather_out(1, h)

    for d in range(2):
        for h in range(2):
            arrived(totals.at[d, h], freq_recv.at[5 + 2 * d + h])
            for a in range(16):
                image_ref[d, 8 * h : 8 * h + 8, 128 * a : 128 * (a + 1)] = totals[d, h, a // 2, a % 2]

    for k in range(6):
        for h in range(2):
            left_here(sent.at[k, h], send_sem.at[k, h])
    left_here(vel_sent, small_send.at[0])
    left_here(img_sent, small_send.at[1])
    shared_left(vel_all, freq_send.at[0])
    for d in range(2):
        for h in range(2):
            shared_left(shares.at[d, h], freq_send.at[1 + 2 * d + h])
            shared_left(totals.at[d, h], freq_send.at[5 + 2 * d + h])


def scratch():
    def vmem(*shape, dtype=F32):
        return pltpu.VMEM(shape, dtype)

    def dma(*shape):
        return pltpu.SemaphoreType.DMA(shape)

    state = (2, 512, 128)
    return [
        vmem(1, 2, 2, 16, NX),
        vmem(2, 16, 256),
        vmem(1, 2, 128, 128),
        vmem(1, 2, 128, 128),
        vmem(128, 768, dtype=BF16),
        vmem(2, 512, 128),
        vmem(768, 256, dtype=BF16),
        vmem(2, 256, 768, dtype=BF16),
        vmem(2, 2, 512, 128),
        vmem(6, *state),
        vmem(6, *state),
        vmem(*state),
        vmem(*state),
        vmem(2, 768, 512, dtype=BF16),
        vmem(768, 128),
        vmem(2, 528, 128),
        vmem(768, 256, dtype=BF16),
        vmem(128, 768, dtype=BF16),
        vmem(2, *state),
        vmem(2, *state),
        vmem(2, *state),
        vmem(2, *state),
        vmem(2, *state),
        vmem(2, *state),
        vmem(GROUPS, 2, 16, 256),
        vmem(512, 128),
        vmem(512, 128),
        vmem(512, 128),
        vmem(512, 128),
        vmem(2, 2, 16, 8, 128),
        vmem(2, 2, GROUPS, 2, 8, 128),
        vmem(2, 2, 2, 8, 128),
        vmem(2, 2, GROUPS, 2, 8, 128),
        dma(6, 2),
        dma(6, 2),
        dma(2),
        dma(2),
        dma(9),
        dma(9),
        dma(9),
    ]


def body(wavefield, velocity, reference_velocity, frequencies, block_x, block_y):
    vmem, smem = pl.BlockSpec(memory_space=pltpu.VMEM), pl.BlockSpec(memory_space=pltpu.SMEM)
    anywhere = pl.BlockSpec(memory_space=pl.ANY)
    constants = [jnp.asarray(t) for t in tables()]
    call = pl.pallas_call(
        kernel,
        out_shape=(
            jax.ShapeDtypeStruct(wavefield.shape, F32),
            jax.ShapeDtypeStruct((2, 16, NX), F32),
        ),
        in_specs=[smem, smem] + [anywhere] * (4 + len(constants)),
        out_specs=(vmem, vmem),
        scratch_shapes=scratch(),
        compiler_params=pltpu.CompilerParams(
            collective_id=0, has_side_effects=True, vmem_limit_bytes=60 * 1024 * 1024
        ),
    )
    return call(reference_velocity, frequencies, wavefield, velocity, block_x, block_y, *constants)


def solution(mesh):
    in_specs = (
        P("freq", None, None, "slab", None),
        P(None, "slab", "freq"),
        P(),
        P("freq"),
        P("freq", None, None, None),
        P("freq", None, None, None),
    )
    out_specs = (P("freq", None, None, "slab", None), P(None, "slab", None))
    return jax.shard_map(body, mesh=mesh, in_specs=in_specs, out_specs=out_specs, check_vma=False)
```
